32 devices in a mesh: chan: 4 (over z), rows: 8 (over y, x, core).
Axes of the slice: x: 2, y: 2, z: 4, core: 2. Of those that a mesh axis runs over, the one named last changes fastest.
Arguments:
- tokens: bfloat16 [512, 512, 512], P('rows', None, 'chan'), may hold values from -60 to 60
- gain_in: float32 [512], P('chan'), may hold values from 0.1 to 1.9
- spectral_w1: float32 [2, 8, 64, 64], P(None, 'chan'), may hold values from -0.75 to 0.75
- spectral_b1: float32 [2, 8, 64], P(None, 'chan'), may hold values from -3 to 3
- spectral_w2: float32 [2, 8, 64, 64], P(None, 'chan'), may hold values from -0.75 to 0.75
- spectral_b2: float32 [2, 8, 64], P(None, 'chan'), may hold values from -3 to 3
- gain_out: float32 [512], replicated, may hold values from 0.1 to 1.9
- fc1_weight: bfloat16 [512, 2048], P(None, 'chan'), may hold values from -0.25 to 0.25
- fc1_bias: bfloat16 [2048], P('chan'), may hold values from -3 to 3
- fc2_weight: bfloat16 [2048, 512], P('chan'), may hold values from -0.1875 to 0.1875
- fc2_bias: bfloat16 [512], P('chan'), may hold values from -3 to 3
Outputs:
- block_out: bfloat16 [512, 512, 512], P('rows', None, 'chan')
The draws below stay inside these ranges and needn't reach their ends.
All inputs are finite; a program needn't handle non-finite values.
Results may differ from the reference program's by a relative error of at most 0.0055.
Values may be sent and summed in bfloat16 or wider, within the bound.
A program may use at most 192 MiB of HBM per device.

```python
from functools import partial
import jax
import jax.numpy as jnp
from jax import lax

HEIGHT = 512
WIDTH = 512
DIM = 512
BLOCKS = 8
FFN = 2048
BLOCK = 64


def draw_tokens(key, part):
    key_base, key_chan, key_token, key_shift = jax.random.split(key, 4)
    ramp = 3.0 ** (jnp.arange(DIM, dtype=jnp.float32) / DIM)
    chan_scale = jnp.exp(jax.random.uniform(key_chan, (DIM,), jnp.float32, jnp.log(0.3), 0.0)) * ramp
    token_scale = jnp.exp(jax.random.uniform(key_token, (HEIGHT, WIDTH, 1), jnp.float32, 0.0, jnp.log(3.0)))
    base = jax.random.normal(key_base, (HEIGHT, WIDTH, DIM), jnp.float32)
    shift = 0.5 * jax.random.normal(key_shift, (DIM,), jnp.float32)
    base = jnp.clip(base, -5.0, 5.0)
    shift = jnp.clip(shift, -3.0, 3.0)
    return ((base * token_scale + shift) * chan_scale).astype(jnp.bfloat16)


def raised(values, rng, source, target, blocks, factor):
    def block_of(dim):
        return (jnp.arange(values.shape[dim]) // (values.shape[dim] // blocks)).reshape((-1,) + (1,) * (values.ndim - 1 - dim))

    one_side = jax.random.permutation(rng, blocks)[block_of(target)]
    other_side = (block_of(target) + blocks // 2) % blocks
    return jnp.where((block_of(source) == one_side) | (block_of(source) == other_side), factor * values, values)


def block_scale(own_key, extent, shards, smallest, high):
    level = 1.0
    for position, shards_of in shards:
        draws = jax.random.uniform(jax.random.fold_in(jax.random.fold_in(own_key, 6), position), (shards_of,), jnp.float32, smallest / len(shards), high / len(shards))
        level = level * jnp.repeat(jnp.exp(draws), extent[position] // shards_of).reshape((-1,) + (1,) * (len(extent) - 1 - position))
    return level


def bell_draw(own_key, extent, scale, limit, pieces=(), kind=jnp.bfloat16):
    values = scale * jax.random.normal(own_key, extent, jnp.float32)
    if pieces:
        values = values * block_scale(own_key, extent, pieces, -0.22, 0.18)
    return jnp.clip(values, -limit, limit).astype(kind)


def noise_with(key, shape, scale, limit, shards, heavy, kind=jnp.bfloat16):
    drawn = scale * jax.random.normal(key, shape, jnp.float32)
    if shards:
        drawn = drawn * block_scale(key, shape, shards, -0.22, 0.18)
    return jnp.clip(raised(drawn, jax.random.fold_in(key, 3), *heavy), -limit, limit).astype(kind)


def setup_inputs(seed: int = 0) -> dict:
    splits = jax.random.split(jax.random.key(seed), 12)
    return {
        "tokens": draw_tokens(jax.random.fold_in(splits[11], 71), 0),
        "gain_in": jnp.clip(1.0 + 0.18 * jax.random.normal(splits[1], (DIM,), jnp.float32), 0.1, 1.9),
        "spectral_w1": bell_draw(splits[2], (2, BLOCKS, BLOCK, BLOCK), BLOCK ** -0.5, 0.75, ((1, 4),), jnp.float32),
        "spectral_b1": bell_draw(splits[3], (2, BLOCKS, BLOCK), 0.5, 3.0, ((1, 4),), jnp.float32),
        "spectral_w2": bell_draw(splits[4], (2, BLOCKS, BLOCK, BLOCK), BLOCK ** -0.5, 0.75, ((1, 4),), jnp.float32),
        "spectral_b2": bell_draw(splits[5], (2, BLOCKS, BLOCK), 0.5, 3.0, ((1, 4),), jnp.float32),
        "gain_out": jnp.clip(1.0 + 0.18 * jax.random.normal(splits[6], (DIM,), jnp.float32), 0.1, 1.9),
        "fc1_weight": bell_draw(splits[7], (DIM, FFN), DIM ** -0.5, 0.25, ((1, 4),)),
        "fc1_bias": bell_draw(splits[8], (FFN,), 0.5, 3.0, ((0, 4),)),
        "fc2_weight": noise_with(splits[9], (FFN, DIM), FFN ** -0.5, 0.1875, ((0, 4),), (0, 1, 4, 2.0)),
        "fc2_bias": bell_draw(splits[10], (DIM,), 0.5, 3.0, ((0, 4),)),
    }


norm_eps = 1e-05
shrink_level = 0.01
highest = lax.Precision.HIGHEST

def normalize(values, gain):
    center = lax.optimization_barrier(jnp.mean(values, axis=-1, keepdims=True))
    spread = lax.optimization_barrier(jnp.mean(values * values, axis=-1, keepdims=True)) - center * center
    return (values - center) * lax.rsqrt(spread + norm_eps) * gain

def soften(values):
    return jnp.where(values > shrink_level, values - shrink_level, jnp.where(values < -shrink_level, values + shrink_level, 0.0))

def block_layer(real_part, imag_part, weights, biases):
    product = partial(jnp.einsum, 'hknb,nbo->hkno', precision=highest)
    weights = weights.astype(jnp.float32)
    return (product(real_part, weights[0]) - product(imag_part, weights[1]) + biases[0], product(imag_part, weights[0]) + product(real_part, weights[1]) + biases[1])

def feed_forward(token_block, gain_out, fc1_weight, fc1_bias, fc2_weight, fc2_bias):
    source = token_block.astype(jnp.float32)
    normed = normalize(source, gain_out).astype(jnp.bfloat16)
    hidden = jax.nn.gelu(jnp.dot(normed, fc1_weight, preferred_element_type=jnp.float32) + fc1_bias.astype(jnp.float32), approximate=False).astype(jnp.bfloat16)
    summed = jnp.dot(hidden, fc2_weight, preferred_element_type=jnp.float32)
    return (source + summed + fc2_bias.astype(jnp.float32)).astype(jnp.bfloat16)

def reference(tokens, gain_in, spectral_w1, spectral_b1, spectral_w2, spectral_b2, gain_out, fc1_weight, fc1_bias, fc2_weight, fc2_bias):
    source = tokens.astype(jnp.float32)
    normed = normalize(source, gain_in)
    spectrum = jnp.fft.rfft2(normed, axes=(0, 1), norm='ortho')[:, :WIDTH // 2, :]
    real_part = jnp.real(spectrum).astype(jnp.float32).reshape(HEIGHT, WIDTH // 2, BLOCKS, BLOCK)
    imag_part = jnp.imag(spectrum).astype(jnp.float32).reshape(HEIGHT, WIDTH // 2, BLOCKS, BLOCK)
    first_real, first_imag = block_layer(real_part, imag_part, spectral_w1, spectral_b1)
    first_real = jnp.maximum(first_real, 0.0)
    first_imag = jnp.maximum(first_imag, 0.0)
    second_real, second_imag = block_layer(first_real, first_imag, spectral_w2, spectral_b2)
    shrunk_real = soften(second_real).reshape(HEIGHT, WIDTH // 2, DIM)
    shrunk_imag = soften(second_imag).reshape(HEIGHT, WIDTH // 2, DIM)
    combined = lax.complex(shrunk_real, shrunk_imag)
    combined = jnp.pad(combined, ((0, 0), (0, 1), (0, 0)))
    filtered = jnp.fft.irfft2(combined, s=(HEIGHT, WIDTH), axes=(0, 1), norm='ortho').astype(jnp.float32)
    mixed = (filtered + normed + source).astype(jnp.bfloat16)
    blocks = mixed.reshape(64, -1, DIM)

    def one_block(token_block):
        return feed_forward(token_block, gain_out, fc1_weight, fc1_bias, fc2_weight, fc2_bias)
    result = lax.map(one_block, blocks)
    return result.reshape(HEIGHT, WIDTH, DIM)
```

```python
import functools
import math

import jax
import jax.numpy as jnp
import numpy as np
from jax import lax
from jax.experimental import pallas as pl
from jax.experimental.pallas import tpu as pltpu
from jax.sharding import PartitionSpec as P

norm_eps = 1e-05
shrink_level = 0.01
spectral_chunks = 2
mlp_chunks = 4
bf16 = jnp.bfloat16
f32 = jnp.float32


def soften(values):
    return values - jnp.clip(values, -shrink_level, shrink_level)


def dft_tables(length):
    index = np.arange(length, dtype=np.int64)
    angle = 2.0 * np.pi / length * (index[:, None] * index[None, :] % length)
    scale = 1.0 / math.sqrt(length)
    return np.cos(angle) * scale, np.sin(angle) * scale


def dot(left, right):
    return jnp.dot(left, right, preferred_element_type=f32)


def spectral_kernel(x_ref, cos_ref, sin_ref, w1_ref, b1_ref, w2_ref, b2_ref, *rest):
    out_ref = rest[-1]
    parts, _, rows, lanes = x_ref.shape
    half = lanes // 2
    x = x_ref[...].reshape(parts * rows, lanes)
    turned = jnp.concatenate([x[:, half:], -x[:, :half]], axis=1)
    spectrum = dot(cos_ref[...], x) + dot(sin_ref[...], turned)
    first = jnp.maximum(dot(spectrum.astype(bf16), w1_ref[...]) + b1_ref[...], 0.0)
    second = dot(first.astype(bf16), w2_ref[...]) + b2_ref[...]
    shrunk = soften(second).astype(bf16)
    turned = jnp.concatenate([-shrunk[:, half:], shrunk[:, :half]], axis=1)
    back = dot(cos_ref[...], shrunk) + dot(sin_ref[...], turned)
    pieces, _, _, piece_rows, _ = out_ref.shape
    back = back.astype(bf16).reshape(parts, pieces, piece_rows, lanes)
    for i in range(pieces):
        out_ref[i, :, 0] = back[:, i]


def spectral_stage(x, cos_table, sin_table, w1, b1, w2, b2, pieces, own, first, held):
    parts, freqs, rows, lanes = x.shape
    length = parts * rows

    def whole(shape):
        return pl.BlockSpec(shape, lambda k: (0,) * len(shape))

    extra = [] if held is None else [held]
    return pl.pallas_call(
        spectral_kernel,
        grid=(freqs,),
        in_specs=[
            pl.BlockSpec((parts, 1, rows, lanes), lambda k: (0, k, 0, 0)),
            whole((length, length)),
            whole((length, length)),
            whole((lanes, lanes)),
            whole((1, lanes)),
            whole((lanes, lanes)),
            whole((1, lanes)),
        ]
        + [pl.BlockSpec(memory_space=pl.ANY)] * len(extra),
        out_specs=pl.BlockSpec(
            (pieces, parts, 1, rows // pieces, lanes), lambda k: (0, 0, first + k, 0, 0)
        ),
        out_shape=jax.ShapeDtypeStruct((pieces, parts, own, rows // pieces, lanes), bf16),
        input_output_aliases={7: 0} if extra else {},
        compiler_params=pltpu.CompilerParams(vmem_limit_bytes=32 * 2**20),
        cost_estimate=pl.CostEstimate(
            flops=freqs * (8 * length * length * lanes + 4 * length * lanes * lanes),
            bytes_accessed=4 * x.size,
            transcendentals=0,
        ),
    )(x, cos_table, sin_table, w1, b1, w2, b2, *extra)


def mlp_kernel(count, *refs):
    x_refs, (gain_ref, w1_ref, b1_ref, w2_ref), out_refs = (
        refs[:count],
        refs[count : count + 4],
        refs[count + 4 :],
    )
    x = jnp.concatenate([ref[...] for ref in x_refs], axis=1).astype(f32)
    center = jnp.mean(x, axis=-1, keepdims=True)
    spread = jnp.mean(x * x, axis=-1, keepdims=True) - center * center
    normed = ((x - center) * lax.rsqrt(spread + norm_eps) * gain_ref[...]).astype(bf16)
    total = None
    for i in range(w1_ref.shape[0]):
        hidden = dot(normed, w1_ref[i]) + b1_ref[i].astype(f32)
        hidden = (0.5 * hidden * (1.0 + lax.erf(hidden * (1.0 / math.sqrt(2.0))))).astype(bf16)
        term = dot(hidden, w2_ref[i])
        total = term if total is None else total + term
    for i, ref in enumerate(out_refs):
        chan = ref.shape[1]
        ref[...] = total[:, i * chan : (i + 1) * chan].astype(bf16)


def mlp_stage(pieces, gain, w1, b1, w2):
    tokens, chan = pieces[0].shape
    count = len(pieces)
    step = min(512, tokens)
    block = pl.BlockSpec((step, chan), lambda t: (t, 0))

    def whole(array):
        return pl.BlockSpec(array.shape, lambda t: (0,) * array.ndim)

    return pl.pallas_call(
        functools.partial(mlp_kernel, count),
        grid=(tokens // step,),
        in_specs=[block] * count + [whole(gain), whole(w1), whole(b1), whole(w2)],
        out_specs=[block] * count,
        out_shape=[jax.ShapeDtypeStruct((tokens, chan), bf16)] * count,
        compiler_params=pltpu.CompilerParams(vmem_limit_bytes=40 * 2**20),
        cost_estimate=pl.CostEstimate(
            flops=4 * tokens * w1.size,
            bytes_accessed=4 * count * tokens * chan,
            transcendentals=0,
        ),
    )(*pieces, gain, w1, b1, w2)


def layer_matrix(weights):
    count, size = weights.shape[1], weights.shape[2]
    eye = jnp.eye(count, dtype=weights.dtype)
    real, imag = (
        (part[:, :, None, :] * eye[:, None, :, None]).reshape(count * size, count * size)
        for part in (weights[0], weights[1])
    )
    return jnp.concatenate(
        [jnp.concatenate([real, imag], 1), jnp.concatenate([-imag, real], 1)], 0
    ).astype(bf16)


def local(
    tokens,
    gain_in,
    spectral_w1,
    spectral_b1,
    spectral_w2,
    spectral_b2,
    gain_out,
    fc1_weight,
    fc1_bias,
    fc2_weight,
    fc2_bias,
):
    row_count, width, chan = tokens.shape
    row_parts = lax.axis_size("rows")
    chan_parts = lax.axis_size("chan")
    all_channels = chan * chan_parts
    height = row_count * row_parts
    half = width // 2
    own = half // row_parts

    source = tokens.astype(f32)
    totals, squares = lax.psum((jnp.sum(source, axis=2), jnp.sum(source * source, axis=2)), "chan")
    fc1_weight, fc2_weight, fc1_bias, totals = lax.optimization_barrier(
        (fc1_weight, fc2_weight, fc1_bias, totals)
    )
    fc1_full = lax.all_gather(fc1_weight, "chan")
    fc2_full = lax.all_gather(fc2_weight, "chan")
    bias_full = lax.all_gather(fc1_bias[None, :], "chan")
    center = (totals / all_channels)[:, :, None]
    spread = (squares / all_channels)[:, :, None] - center * center
    normed = (source - center) * lax.rsqrt(spread + norm_eps) * gain_in
    normed_low = normed.astype(bf16)

    cos_w, sin_w = dft_tables(width)
    cos_h, sin_h = dft_tables(height)
    forward = np.stack([cos_w[:half], -sin_w[:half]], 1)
    weighting = np.where(np.arange(half) == 0, 1.0, 2.0)[:, None, None]
    inverse = forward * weighting
    shape = (row_parts, spectral_chunks, own // spectral_chunks, 2, width)
    forward = jnp.asarray(forward.reshape(shape), bf16)
    inverse = jnp.asarray(inverse.reshape(shape), bf16)
    cos_h = jnp.asarray(cos_h, bf16)
    sin_h = jnp.asarray(sin_h, bf16)
    w1, w2 = layer_matrix(spectral_w1), layer_matrix(spectral_w2)
    b1, b2 = spectral_b1.reshape(1, -1), spectral_b2.reshape(1, -1)

    pieces = max(1, min(mlp_chunks, row_count // 16))
    rows = row_count // pieces
    group = own // spectral_chunks
    back = None
    for j in range(spectral_chunks):
        spectra = jnp.einsum(
            "rwc,dkpw->dkrpc", normed_low, forward[:, j], preferred_element_type=f32
        ).astype(bf16)
        spectra = spectra.reshape(row_parts, group, row_count, 2 * chan)
        columns = lax.all_to_all(spectra, "rows", split_axis=0, concat_axis=0, tiled=True)
        if j == spectral_chunks - 1:
            columns, fc1_full, fc2_full, bias_full = lax.optimization_barrier(
                (columns, fc1_full, fc2_full, bias_full)
            )
        back = spectral_stage(
            columns, cos_h, sin_h, w1, b1, w2, b2, pieces, own, j * group, back
        )

    me = lax.axis_index("chan")

    def turned(values, axis):
        starts = [lax.rem(me + chan_parts - s, chan_parts) * chan for s in range(chan_parts)]
        blocks = [lax.dynamic_slice_in_dim(values, start, chan, axis) for start in starts]
        return jnp.concatenate(blocks, axis)

    gain_turned = turned(gain_out, 0).reshape(1, all_channels)
    fc1_turned = turned(fc1_full, 1)
    fc2_turned = turned(fc2_full, 2)
    part = width // chan_parts
    places = [lax.rem(me + s, chan_parts) * part for s in range(chan_parts)]

    def turn(values, shift):
        if shift % chan_parts == 0:
            return values
        pairs = [(i, (i + shift) % chan_parts) for i in range(chan_parts)]
        return lax.ppermute(values, "chan", pairs)

    out = jnp.zeros(tokens.shape, bf16)
    table = inverse.reshape(row_parts, own, 2, width)
    for j in range(pieces):
        returned = lax.all_to_all(back[j], "rows", split_axis=0, concat_axis=0, tiled=True)
        returned = returned.reshape(row_parts, own, rows, 2, chan)
        filtered = jnp.einsum("dkrpc,dkpw->rwc", returned, table, preferred_element_type=f32)
        span = slice(j * rows, (j + 1) * rows)
        mixed = (filtered + normed[span] + source[span]).astype(bf16)
        kept = [lax.dynamic_slice_in_dim(mixed, place, part, 1) for place in places]
        full = [turn(kept[s].reshape(rows * part, chan), s) for s in range(chan_parts)]
        done = mlp_stage(full, gain_turned, fc1_turned, bias_full, fc2_turned)
        for s in range(chan_parts):
            summed = turn(done[s], -s).reshape(rows, part, chan)
            final = (kept[s].astype(f32) + summed.astype(f32) + fc2_bias.astype(f32)).astype(bf16)
            out = lax.dynamic_update_slice(out, final, (j * rows, places[s], 0))
    return out


def solution(mesh):
    return jax.shard_map(
        local,
        mesh=mesh,
        in_specs=(
            P("rows", None, "chan"),
            P("chan"),
            P(None, "chan", None, None),
            P(None, "chan", None),
            P(None, "chan", None, None),
            P(None, "chan", None),
            P(),
            P(None, "chan"),
            P("chan"),
            P("chan", None),
            P("chan"),
        ),
        out_specs=P("rows", None, "chan"),
        check_vma=False,
    )
```
